32 devices in a mesh: lat: 4 (over y, x), lon: 8 (over z, core).
Axes of the slice: x: 2, y: 2, z: 4, core: 2. Of those that a mesh axis runs over, the one named last changes fastest.
Arguments:
- tokens: bfloat16 [32, 256, 1024], P('lat', 'lon'), may hold values from -40 to 40
- ln_gain: float32 [1024], replicated, may hold values from 0.1 to 1.9
- w_qkv: bfloat16 [1024, 1536], replicated, may hold values from -0.34375 to 0.34375
- bias_table: float32 [8, 225], replicated, may hold values from -4 to 4
- bias_index: int32 [64, 64], replicated, may hold values from 0 to 224
- cap_group: int32 [2, 64, 4, 1], P(None, 'lon'), may hold values from 0 to 7; in each aligned block of 32 rows (0 to 31, 32 to 63, ..., all dimensions but the last counted through in order) at most 8 rows name the same one
Outputs:
- mixed: bfloat16 [32, 256, 512], P('lat', 'lon')
The draws below stay inside these ranges and needn't reach their ends.
Inputs may be any that keep to these rules, and one draw needn't show every extreme that they name: `cap_group`: within one pole, the 32 tiles of one longitude sector name any one group at most 8 times, and some sector names some group exactly 8 times.
All inputs are finite; a program needn't handle non-finite values.
Results may differ from the reference program's by a relative error of at most 0.0079.
Values may be sent and summed in bfloat16 or wider, within the bound.
A program may use at most 128 MiB of HBM per device.

```python
import math
import jax
import jax.numpy as jnp
import numpy as np
from jax import lax

D = 1024
HEADS = 8
HD = 64
WIN = 8
TW = 4
CAP = 4
HW = 512
HALF = 4
BIAS_ROWS = 225
H = 32
W = 256
TCOLS = 64
TILES_DEV = 32
MOST = 8
N_LON = 8


def draw_tokens(key, part):
    key_rows, key_cols, key_main = jax.random.split(key, 3)
    low = math.log(0.3)
    high = math.log(3.0)
    row_scale = jnp.exp(jax.random.uniform(key_rows, (H, W, 1), jnp.float32, low, high))
    col_scale = jnp.exp(jax.random.uniform(key_cols, (D,), jnp.float32, low, high))
    base = jnp.clip(jax.random.normal(key_main, (H, W, D), jnp.float32), -4.0, 4.0)
    return (base * row_scale * col_scale).astype(jnp.bfloat16)


def draw_w_qkv(key, part):
    key_main = jax.random.fold_in(jax.random.fold_in(key, 7), 0)
    full = jnp.clip(jax.random.normal(key_main, (D, 3 * HW), jnp.float32), -4.0, 4.0) * D ** (-0.5)
    return full.astype(jnp.bfloat16)


def touch_ends(entries, rng, least, top_value):
    spot = [jax.random.randint(jax.random.fold_in(rng, axis), (), 0, length) for axis, length in enumerate(entries.shape)]
    main_axis = entries.shape.index(max(entries.shape))
    neighbour = spot[:main_axis] + [(spot[main_axis] + 1) % entries.shape[main_axis]] + spot[main_axis + 1:]
    return entries.at[tuple(spot)].set(least).at[tuple(neighbour)].set(top_value)


def shared_out(rng, own, number, rows, number_of, top, most, slope):
    ranking = jax.random.permutation(rng, number_of)
    crowded, usual = load_shares(number_of, rows * top, most, slope, True), load_shares(number_of, rows * top, most, slope, False)
    places = jnp.arange(number_of)

    def named(tallies, turn):
        used = int((tallies > 0).sum())
        fixed = max(1, used // 4)
        moved = fixed + (places - fixed + turn * (used - fixed)) % max(1, number_of - fixed)
        return jnp.zeros((number_of,), jnp.int32).at[ranking[jnp.where(places < fixed, places, moved)]].set(jnp.asarray(tallies, jnp.int32))

    tallies = jnp.where(number % 4 == 0, named(crowded, number // 4), named(usual, number - number // 4 - 1))
    mixed = jax.random.permutation(jax.random.fold_in(own, 3), number_of)
    donor, taker = mixed[0:number_of // 2 * 2:2], mixed[1:number_of // 2 * 2:2]
    room = jnp.minimum(tallies[donor] - 1, most - tallies[taker]) // 2
    room = jnp.where((donor == ranking[0]) | (taker == ranking[0]) | (tallies[taker] == 0), 0, jnp.maximum(room, 0))
    moved = jax.random.randint(jax.random.fold_in(own, 4), (number_of // 2,), 0, 1 << 20) % (room + 1)
    tallies = tallies.at[donor].add(-moved).at[taker].add(moved)
    members = jnp.searchsorted(jnp.cumsum(tallies), jnp.arange(rows * top), side="right").astype(jnp.int32)
    table = members.reshape(top, rows).T
    table = table[jax.random.permutation(jax.random.fold_in(own, 1), rows)]
    turn = jax.random.randint(jax.random.fold_in(own, 2), (rows, 1), 0, top)
    return jnp.take_along_axis(table, (jnp.arange(top)[None, :] + turn) % top, axis=1)


def load_shares(count, total, most, skew, full):
    loads = [(1 << 20) // math.isqrt(standing ** skew) + 1 for standing in range(1, count + 1)]
    largest = most if full else min(most, max(-(-total // count), total * loads[0] // sum(loads)))
    least = 1 if total - largest >= count - 1 else 0
    holding, spare = [largest] + [least] * (count - 1), total - largest - least * (count - 1)
    while spare > 0:
        movable = [i for i in range(1, count) if holding[i] < largest] or [i for i in range(1, count) if holding[i] < most]
        pool, remaining = sum([loads[i] for i in movable]), spare
        for i in movable:
            more = min(most - holding[i], max(1, remaining * loads[i] // pool), spare)
            holding[i] = holding[i] + more
            spare = spare - more
    return np.array(holding)


def centred(own_key, extent, deviation, limit, kind=jnp.bfloat16):
    drawn = jax.random.normal(own_key, extent, jnp.float32) * deviation
    return jnp.minimum(jnp.maximum(drawn, -limit), limit).astype(kind)


def setup_inputs(seed: int = 0) -> dict:
    key_list = jax.random.split(jax.random.key(seed), 7)
    tokens = draw_tokens(jax.random.fold_in(key_list[6], 71), 0)
    ln_gain = jnp.clip(1.0 + 0.18 * jax.random.normal(key_list[1], (D,), jnp.float32), 0.1, 1.9)
    w_qkv = draw_w_qkv(jax.random.fold_in(key_list[6], 71), 0)
    bias_table = centred(key_list[3], (HEADS, BIAS_ROWS), 1.0, 4.0, jnp.float32)
    bias_index = touch_ends(jax.random.randint(key_list[4], (WIN * WIN, WIN * WIN), 0, BIAS_ROWS), jax.random.fold_in(key_list[4], 1), 0, BIAS_ROWS - 1).astype(jnp.int32)
    cap_group_keys = jax.random.split(jax.random.fold_in(key_list[5], 1), 2 * TCOLS * CAP // TILES_DEV)
    cap_group_turns = jax.random.permutation(jax.random.fold_in(key_list[5], 3), 2 * TCOLS * CAP // TILES_DEV)
    cap_group = jax.vmap(lambda own, number: shared_out(jax.random.fold_in(key_list[5], 2), own, number, TILES_DEV, N_LON, 1, MOST, 2))(cap_group_keys, cap_group_turns).reshape((2, TCOLS, CAP, 1))
    return dict(tokens=tokens, ln_gain=ln_gain, w_qkv=w_qkv, bias_table=bias_table, bias_index=bias_index, cap_group=cap_group)


epsilon = 1e-05
masked_score = -1e+30

def layer_norm(row_tokens, ln_gain):
    values = row_tokens.astype(jnp.float32)
    center = lax.optimization_barrier(jnp.mean(values, axis=-1, keepdims=True))
    spread = lax.optimization_barrier(jnp.mean(jnp.square(values - center), axis=-1, keepdims=True))
    return ((values - center) * lax.rsqrt(spread + epsilon) * ln_gain).astype(jnp.bfloat16)

def softmax_bf16(scores):
    highest = lax.optimization_barrier(jnp.max(scores, axis=-1, keepdims=True))
    raised = jnp.exp(scores - highest)
    return (raised / lax.optimization_barrier(jnp.sum(raised, axis=-1, keepdims=True))).astype(jnp.bfloat16)

def reference(tokens, ln_gain, w_qkv, bias_table, bias_index, cap_group):
    att_scale = HD ** (-0.5)

    def project_row(row_tokens):
        return jnp.dot(layer_norm(row_tokens, ln_gain), w_qkv, preferred_element_type=jnp.float32).astype(jnp.bfloat16)
    projected = lax.map(project_row, tokens)
    position_bias = bias_table[:, bias_index]
    shifted = jnp.roll(projected, HALF, axis=1)
    padded = jnp.pad(shifted, ((HALF, HALF), (0, 0), (0, 0)))
    strip_count = (H + WIN) // WIN
    strips = padded.reshape(strip_count, WIN, W, 3 * HW)

    def strip_attention(strip_item):
        strip_rows, strip_index = strip_item
        windows = strip_rows.reshape(WIN, W // WIN, WIN, 3 * HW).transpose(1, 0, 2, 3)
        windows = windows.reshape(W // WIN, WIN * WIN, 3 * HW).astype(jnp.float32)
        win_q = windows[:, :, :HW].reshape(-1, WIN * WIN, HEADS, HD)
        win_k = windows[:, :, HW:2 * HW].reshape(-1, WIN * WIN, HEADS, HD)
        win_v = windows[:, :, 2 * HW:].reshape(-1, WIN * WIN, HEADS, HD)
        scores = jnp.einsum('wqhd,wkhd->whqk', win_q, win_k) * att_scale + position_bias[None]
        row_pos = strip_index * WIN + jnp.arange(WIN * WIN, dtype=jnp.int32) // WIN
        valid = (row_pos >= HALF) & (row_pos < H + HALF)
        scores = jnp.where(valid[None, None, None, :], scores, masked_score)
        weights = softmax_bf16(scores).astype(jnp.float32)
        mixed_out = jnp.einsum('whqk,wkhd->wqhd', weights, win_v)
        mixed_out = mixed_out.reshape(W // WIN, WIN, WIN, HW).transpose(1, 0, 2, 3)
        return mixed_out.reshape(WIN, W, HW)
    win_strips = lax.map(strip_attention, (strips, jnp.arange(strip_count, dtype=jnp.int32)))
    win_out = win_strips.reshape(H + WIN, W, HW)[HALF:HALF + H]
    win_out = jnp.roll(win_out, -HALF, axis=1)

    def cap_pole(pole_rows, groups):
        token_group = jnp.repeat(groups.T, TW, axis=1).reshape(-1)
        flat_rows = pole_rows.reshape(CAP * W, 3 * HW).astype(jnp.float32)
        cap_keys = flat_rows[:, HW:2 * HW].reshape(-1, HEADS, HD)
        cap_values = flat_rows[:, 2 * HW:].reshape(-1, HEADS, HD)
        block_rows = math.gcd(CAP * W, 512)

        def one_block(block_start):
            query_block = lax.dynamic_slice_in_dim(flat_rows, block_start, block_rows, 0)[:, :HW]
            query_block = query_block.reshape(block_rows, HEADS, HD)
            group_block = lax.dynamic_slice_in_dim(token_group, block_start, block_rows, 0)
            scores = jnp.einsum('qhd,khd->hqk', query_block, cap_keys) * att_scale
            same_group = group_block[:, None] == token_group[None, :]
            scores = jnp.where(same_group[None], scores, masked_score)
            weights = softmax_bf16(scores).astype(jnp.float32)
            return jnp.einsum('hqk,khd->qhd', weights, cap_values).reshape(block_rows, HW)
        block_starts = jnp.arange(0, CAP * W, block_rows, dtype=jnp.int32)
        return lax.map(one_block, block_starts).reshape(CAP, W, HW).astype(jnp.bfloat16)
    north = cap_pole(projected[:CAP], cap_group[0, :, :, 0])
    south = cap_pole(projected[H - CAP:], cap_group[1, :, :, 0])
    win_out = win_out.at[:CAP].add(north.astype(jnp.float32))
    win_out = win_out.at[H - CAP:].add(south.astype(jnp.float32))
    return win_out.astype(jnp.bfloat16)
```

```python
import functools

import jax
import jax.numpy as jnp
from jax import lax
from jax.experimental import pallas as pl
from jax.experimental.pallas import tpu as pltpu
from jax.sharding import PartitionSpec as P

MESH = pl.DeviceIdType.MESH
HEADS = 8
HD = 64
HW = 512
STRIP = 128
QUAD = 16
EXT = STRIP + 2 * QUAD
PAIRS = HEADS // 2
epsilon = 1e-05
masked_score = -1e30
f32, bf16 = jnp.float32, jnp.bfloat16


def one_hot(rows, columns, source):
    row = lax.broadcasted_iota(jnp.int32, (rows, columns), 0)
    column = lax.broadcasted_iota(jnp.int32, (rows, columns), 1)
    return jnp.where(source(row) == column, 1.0, 0.0).astype(bf16)


def grid_token(n):
    strip, block, row, column = n // STRIP, (n // QUAD) % 8, (n // 4) % 4, n % 4
    return (strip * 4 + row) * 32 + block * 4 + column


def block_token(n):
    row, column = n // 32, n % 32
    return (row // 4) * STRIP + (column // 4) * QUAD + (row % 4) * 4 + column % 4


def window_position(n):
    high, side, row, column = n // 32, (n // QUAD) % 2, (n // 4) % 4, n % 4
    return (high * 4 + row) * 8 + side * 4 + column


def dot(a, b):
    return jnp.dot(a, b, preferred_element_type=f32)


def dot_t(a, b):
    return lax.dot_general(a, b, (((1,), (1,)), ((), ())), preferred_element_type=f32)


def layer_norm(x, gain):
    values = x.astype(f32)
    center = jnp.mean(values, axis=-1, keepdims=True)
    values = values - center
    spread = jnp.mean(values * values, axis=-1, keepdims=True)
    return (values * lax.rsqrt(spread + epsilon) * gain).astype(bf16)


def softmax_bf16(scores):
    raised = jnp.exp(scores - jnp.max(scores, axis=-1, keepdims=True))
    return (raised * (1.0 / jnp.sum(raised, axis=-1, keepdims=True))).astype(bf16)


def swap_halves(x):
    return jnp.concatenate([x[:, HD:], x[:, :HD]], axis=1)


def kernel(
    lat_n, lon_n, x_hbm, gain_ref, w_hbm, table_ref, index_ref, group_ref, out_ref,
    x_ref, w_ref, own, halo, q_ref, kv_ref, bias_ref, cap_send, cap_recv, ret_send, ret_recv, acc,
    load_sem, hs_sem, hr_sem, cs_sem, cr_sem, rs_sem, rr_sem,
):
    lat, lon = lax.axis_index("lat"), lax.axis_index("lon")
    west, east = lax.rem(lon + lon_n - 1, lon_n), lax.rem(lon + 1, lon_n)
    has_n, has_s = lat > 0, lat < lat_n - 1
    polar = (lat == 0) | (lat == lat_n - 1)
    x_copy = pltpu.make_async_copy(x_hbm, x_ref, load_sem.at[0])
    w_copy = pltpu.make_async_copy(w_hbm, w_ref, load_sem.at[1])
    x_copy.start()
    w_copy.start()

    barrier = pltpu.get_barrier_semaphore()

    def greet(a, o):
        pl.semaphore_signal(barrier, inc=1, device_id=(a, o), device_id_type=MESH)

    greet(lat, west)
    greet(lat, east)

    @pl.when(has_n)
    def _():
        for o in (west, lon, east):
            greet(lat - 1, o)

    @pl.when(has_s)
    def _():
        for o in (west, lon, east):
            greet(lat + 1, o)

    @pl.when(polar)
    def _():
        @pl.loop(2, lon_n - 1)
        def _(o):
            greet(lat, lax.rem(lon + o, lon_n))

    x_copy.wait()
    own[...] = dot(one_hot(2 * STRIP, 2 * STRIP, grid_token), x_ref[...]).astype(bf16)

    as_int = lambda flag: jnp.where(flag, 1, 0)
    pl.semaphore_wait(
        barrier, 2 + 3 * as_int(has_n) + 3 * as_int(has_s) + (lon_n - 3) * as_int(polar)
    )

    def halo_copy(slot, source, target, rows, a, o):
        return pltpu.make_async_remote_copy(
            src_ref=own.at[pl.ds(source, rows)],
            dst_ref=halo.at[pl.ds(target, rows)],
            send_sem=hs_sem.at[slot],
            recv_sem=hr_sem.at[slot],
            device_id=(a, o),
            device_id_type=MESH,
        )

    last = STRIP - QUAD
    north = [
        halo_copy(0, 0, EXT + QUAD, STRIP, lat - 1, lon),
        halo_copy(1, 0, EXT + EXT - QUAD, QUAD, lat - 1, west),
        halo_copy(2, last, EXT, QUAD, lat - 1, east),
    ]
    south = [
        halo_copy(3, STRIP, QUAD, STRIP, lat + 1, lon),
        halo_copy(4, STRIP, EXT - QUAD, QUAD, lat + 1, west),
        halo_copy(5, STRIP + last, 0, QUAD, lat + 1, east),
    ]
    sides = [
        halo_copy(6, 0, 2 * EXT + 2 * QUAD, QUAD, lat, west),
        halo_copy(7, STRIP, 2 * EXT + 3 * QUAD, QUAD, lat, west),
        halo_copy(8, last, 2 * EXT, QUAD, lat, east),
        halo_copy(9, STRIP + last, 2 * EXT + QUAD, QUAD, lat, east),
    ]

    @pl.when(has_n)
    def _():
        for c in north:
            c.start()

    @pl.when(has_s)
    def _():
        for c in south:
            c.start()

    for c in sides:
        c.start()

    gain = gain_ref[...]
    normed = layer_norm(own[...], gain)
    w_copy.wait()
    q_ref[...] = (dot(normed, w_ref[:, :HW]).astype(bf16) * HD ** (-0.5)).astype(bf16)
    for part in range(2):
        got = dot(normed, w_ref[:, (part + 1) * HW : (part + 2) * HW]).astype(bf16)
        kv_ref[1, QUAD : QUAD + STRIP, part * HW : (part + 1) * HW] = got[:STRIP]
        kv_ref[2, QUAD : QUAD + STRIP, part * HW : (part + 1) * HW] = got[STRIP:]

    head0 = lax.rem(lon, HEADS)
    base = lon - head0

    def cap_copy(o):
        d = lax.rem(lon + o, lon_n)
        return pltpu.make_async_remote_copy(
            src_ref=cap_send.at[lax.rem(d, HEADS)],
            dst_ref=cap_recv.at[lon],
            send_sem=cs_sem.at[o],
            recv_sem=cr_sem.at[o],
            device_id=(lat, d),
            device_id_type=MESH,
        )

    def ret_copy(j):
        d = base + lax.rem(head0 + j, HEADS)
        return pltpu.make_async_remote_copy(
            src_ref=ret_send.at[j],
            dst_ref=ret_recv.at[head0],
            send_sem=rs_sem.at[j],
            recv_sem=rr_sem.at[j],
            device_id=(lat, d),
            device_id_type=MESH,
        )

    def cap_pack(strip):
        lane = lax.broadcasted_iota(jnp.int32, (4, STRIP), 1)
        row = lax.broadcasted_iota(jnp.int32, (4, STRIP), 0)
        spread = jnp.where((lane // 4) % 4 == row, 1.0, 0.0).astype(bf16)
        ids = dot(group_ref[strip].astype(f32).astype(bf16), spread)
        block = lax.broadcasted_iota(jnp.int32, (8, STRIP), 0)
        where = lax.broadcasted_iota(jnp.int32, (8, STRIP), 1) // QUAD
        ids = jnp.sum(jnp.where(block == where, ids, 0.0), axis=0, keepdims=True)
        ids = jnp.broadcast_to(ids, (QUAD, STRIP)).astype(bf16)
        for h in range(HEADS):
            k = kv_ref[1 + strip, QUAD : QUAD + STRIP, h * HD : (h + 1) * HD]
            v = kv_ref[1 + strip, QUAD : QUAD + STRIP, HW + h * HD : HW + (h + 1) * HD]
            q = q_ref[strip * STRIP : (strip + 1) * STRIP, h * HD : (h + 1) * HD]
            cap_send[h, :STRIP] = jnp.concatenate([k, v], axis=1)
            cap_send[h, STRIP : STRIP + HD] = jnp.concatenate([q[:HD], q[HD:]], axis=1)
            cap_send[h, STRIP + HD :] = ids

    @pl.when(lat == 0)
    def _():
        cap_pack(0)

    @pl.when(lat == lat_n - 1)
    def _():
        cap_pack(1)

    @pl.when(polar)
    def _():
        @pl.loop(1, lon_n)
        def _(o):
            cap_copy(o).start()

        cap_recv[lon] = cap_send[head0]

    order = one_hot(64, 64, window_position)
    index = index_ref[...].astype(f32).astype(bf16)
    index = dot_t(dot(order, index).astype(bf16), order).astype(jnp.int32)
    index = jnp.concatenate([index, index], axis=1)
    table = table_ref[...]
    table_low = table[:, :128]
    table_high = jnp.concatenate(
        [table[:, 128:], jnp.zeros((HEADS, 256 - table.shape[1]), f32)], axis=1
    )
    key = lax.broadcasted_iota(jnp.int32, (64, 64), 1)
    for h in range(HEADS):
        low = jnp.take_along_axis(
            jnp.broadcast_to(table_low[h : h + 1], (64, 128)), index & 127, axis=1,
            mode="promise_in_bounds",
        )
        high = jnp.take_along_axis(
            jnp.broadcast_to(table_high[h : h + 1], (64, 128)), index & 127, axis=1,
            mode="promise_in_bounds",
        )
        bias = jnp.where(index < 128, low, high)[:, :64]
        at = (h % 2) * 32
        north_bias = jnp.where((key < 32) & (lat == 0), masked_score, bias)
        south_bias = jnp.where((key >= 32) & (lat == lat_n - 1), masked_score, bias)
        bias_ref[0, h // 2, at : at + 32] = north_bias[32:]
        bias_ref[1, h // 2, at : at + 32] = south_bias[:32]

    @pl.when(has_n)
    def _():
        for c in south:
            c.wait_recv()

    @pl.when(has_s)
    def _():
        for c in north:
            c.wait_recv()

    for c in sides:
        c.wait_recv()

    @pl.when(jnp.logical_not(has_n))
    def _():
        halo[:EXT] = jnp.zeros((EXT, halo.shape[1]), bf16)

    @pl.when(jnp.logical_not(has_s))
    def _():
        halo[EXT : 2 * EXT] = jnp.zeros((EXT, halo.shape[1]), bf16)

    normed = layer_norm(halo[...], gain)
    for part in range(2):
        columns = slice(part * HW, (part + 1) * HW)
        got = dot(normed, w_ref[:, (part + 1) * HW : (part + 2) * HW]).astype(bf16)
        kv_ref[0, :, columns] = got[:EXT]
        kv_ref[3, :, columns] = got[EXT : 2 * EXT]
        for s in range(2):
            at = 2 * EXT + s * QUAD
            kv_ref[1 + s, :QUAD, columns] = got[at : at + QUAD]
            kv_ref[1 + s, EXT - QUAD :, columns] = got[at + 2 * QUAD : at + 3 * QUAD]

    left = lax.broadcasted_iota(jnp.int32, (1, 128), 1) < HD

    @pl.when(polar)
    def _():
        @pl.loop(1, lon_n)
        def _(o):
            cap_copy(o).wait_recv()

        kv = jnp.concatenate([cap_recv[t, :STRIP] for t in range(lon_n)], axis=0)
        key_group = jnp.concatenate(
            [cap_recv[t, STRIP + HD :].astype(f32)[:1] for t in range(lon_n)], axis=1
        )
        diagonal = lax.broadcasted_iota(jnp.int32, (STRIP, STRIP), 0) == lax.broadcasted_iota(
            jnp.int32, (STRIP, STRIP), 1
        )

        def block(s):
            packed = cap_recv[s, STRIP : STRIP + HD].astype(f32)
            q = jnp.concatenate([packed, swap_halves(packed)], axis=0)
            q = jnp.where(left, q, 0.0).astype(bf16)
            ids = cap_recv[s, STRIP + HD :].astype(f32)[:1]
            group = jnp.sum(jnp.where(diagonal, ids, 0.0), axis=1, keepdims=True)
            scores = jnp.where(group == key_group, dot_t(q, kv), masked_score)
            result = dot(softmax_bf16(scores), kv)
            return jnp.where(left, swap_halves(result[:HD]), result[HD:]).astype(bf16)

        @pl.loop(1, HEADS)
        def _(j):
            ret_send[j] = block(base + lax.rem(head0 + j, HEADS))
            ret_copy(j).start()

        ret_recv[head0] = block(lon)

    keep = [jnp.where(left, 1.0, 0.0).astype(bf16), jnp.where(left, 0.0, 1.0).astype(bf16)]
    for a in range(2):
        for w in range(5):
            if w == 0:
                first, count, skip = 0, QUAD, QUAD
            elif w == 4:
                first, count, skip = STRIP - QUAD, QUAD, 0
            else:
                first, count, skip = QUAD + 32 * (w - 1), 32, 0
            first += a * STRIP
            for pair in range(PAIRS):
                lanes = slice(pair * 128, (pair + 1) * 128)
                v_lanes = slice(HW + pair * 128, HW + (pair + 1) * 128)
                rows = slice(32 * w, 32 * w + 32)
                k = jnp.concatenate([kv_ref[2 * a, rows, lanes], kv_ref[2 * a + 1, rows, lanes]], axis=0)
                v = jnp.concatenate(
                    [kv_ref[2 * a, rows, v_lanes], kv_ref[2 * a + 1, rows, v_lanes]], axis=0
                )
                q = q_ref[first : first + count, lanes]
                q = jnp.concatenate([q * keep[0], q * keep[1]], axis=0)
                bias = jnp.concatenate(
                    [
                        bias_ref[a, pair, skip : skip + count],
                        bias_ref[a, pair, 32 + skip : 32 + skip + count],
                    ],
                    axis=0,
                )
                result = dot(softmax_bf16(dot_t(q, k) + bias), v)
                acc[first : first + count, lanes] = jnp.where(left, result[:count], result[count:])

    def add_cap(strip):
        for pair in range(PAIRS):
            lanes = slice(pair * 128, (pair + 1) * 128)
            even, odd = ret_recv[2 * pair].astype(f32), ret_recv[2 * pair + 1].astype(f32)
            at = strip * STRIP
            acc[at : at + HD, lanes] += jnp.where(left, even, swap_halves(odd))
            acc[at + HD : at + STRIP, lanes] += jnp.where(left, swap_halves(even), odd)

    @pl.when(polar)
    def _():
        @pl.loop(1, HEADS)
        def _(j):
            ret_copy(j).wait_recv()

    @pl.when(lat == 0)
    def _():
        add_cap(0)

    @pl.when(lat == lat_n - 1)
    def _():
        add_cap(1)

    mixed = acc[...].astype(bf16)
    out_ref[...] = dot(one_hot(2 * STRIP, 2 * STRIP, block_token), mixed).astype(bf16)

    @pl.when(has_n)
    def _():
        for c in north:
            c.wait_send()

    @pl.when(has_s)
    def _():
        for c in south:
            c.wait_send()

    for c in sides:
        c.wait_send()

    @pl.when(polar)
    def _():
        @pl.loop(1, lon_n)
        def _(o):
            cap_copy(o).wait_send()

        @pl.loop(1, HEADS)
        def _(j):
            ret_copy(j).wait_send()


def local(tokens, ln_gain, w_qkv, bias_table, bias_index, cap_group):
    lat_n, lon_n = lax.axis_size("lat"), lax.axis_size("lon")
    rows, columns, width = tokens.shape
    count = rows * columns
    vmem = pl.BlockSpec(memory_space=pltpu.VMEM)
    anywhere = pl.BlockSpec(memory_space=pl.ANY)
    out = pl.pallas_call(
        functools.partial(kernel, lat_n, lon_n),
        out_shape=jax.ShapeDtypeStruct((count, HW), bf16),
        in_specs=[anywhere, vmem, anywhere, vmem, vmem, vmem],
        out_specs=vmem,
        scratch_shapes=[
            pltpu.VMEM((count, width), bf16),
            pltpu.VMEM(w_qkv.shape, bf16),
            pltpu.VMEM((count, width), bf16),
            pltpu.VMEM((2 * EXT + 4 * QUAD, width), bf16),
            pltpu.VMEM((count, HW), bf16),
            pltpu.VMEM((4, EXT, 2 * HW), bf16),
            pltpu.VMEM((2, PAIRS, 64, 64), f32),
            pltpu.VMEM((HEADS, STRIP + HD + QUAD, 128), bf16),
            pltpu.VMEM((lon_n, STRIP + HD + QUAD, 128), bf16),
            pltpu.VMEM((HEADS, HD, 128), bf16),
            pltpu.VMEM((HEADS, HD, 128), bf16),
            pltpu.VMEM((count, HW), f32),
            pltpu.SemaphoreType.DMA((2,)),
            pltpu.SemaphoreType.DMA((10,)),
            pltpu.SemaphoreType.DMA((10,)),
            pltpu.SemaphoreType.DMA((lon_n,)),
            pltpu.SemaphoreType.DMA((lon_n,)),
            pltpu.SemaphoreType.DMA((HEADS,)),
            pltpu.SemaphoreType.DMA((HEADS,)),
        ],
        compiler_params=pltpu.CompilerParams(
            collective_id=0, has_side_effects=True, vmem_limit_bytes=48 * 1024 * 1024
        ),
    )(
        tokens.reshape(count, width), ln_gain.reshape(1, width), w_qkv, bias_table, bias_index,
        cap_group.reshape(cap_group.shape[:3]),
    )
    return out.reshape(rows, columns, HW)


def solution(mesh):
    placed = (P("lat", "lon", None), P(), P(), P(), P(), P(None, "lon", None, None))
    return jax.shard_map(
        local, mesh=mesh, in_specs=placed, out_specs=P("lat", "lon", None), check_vma=False
    )
```

```python
import functools

import jax
import jax.numpy as jnp
from jax import lax
from jax.experimental import pallas as pl
from jax.experimental.pallas import tpu as pltpu
from jax.sharding import PartitionSpec as P

MESH = pl.DeviceIdType.MESH
HEADS = 8
HD = 64
HW = 512
STRIP = 128
QUAD = 16
EXT = STRIP + 2 * QUAD
PAIRS = HEADS // 2
epsilon = 1e-05
masked_score = -1e30
f32, bf16 = jnp.float32, jnp.bfloat16


def one_hot(rows, columns, source):
    row = lax.broadcasted_iota(jnp.int32, (rows, columns), 0)
    column = lax.broadcasted_iota(jnp.int32, (rows, columns), 1)
    return jnp.where(source(row) == column, 1.0, 0.0).astype(bf16)


def grid_token(n):
    strip, block, row, column = n // STRIP, (n // QUAD) % 8, (n // 4) % 4, n % 4
    return (strip * 4 + row) * 32 + block * 4 + column


def block_token(n):
    row, column = n // 32, n % 32
    return (row // 4) * STRIP + (column // 4) * QUAD + (row % 4) * 4 + column % 4


def window_position(n):
    high, side, row, column = n // 32, (n // QUAD) % 2, (n // 4) % 4, n % 4
    return (high * 4 + row) * 8 + side * 4 + column


def dot(a, b):
    return jnp.dot(a, b, preferred_element_type=f32)


def dot_t(a, b):
    return lax.dot_general(a, b, (((1,), (1,)), ((), ())), preferred_element_type=f32)


def layer_norm(x, gain):
    values = x.astype(f32)
    center = jnp.mean(values, axis=-1, keepdims=True)
    values = values - center
    spread = jnp.mean(values * values, axis=-1, keepdims=True)
    return (values * lax.rsqrt(spread + epsilon) * gain).astype(bf16)


def softmax_bf16(scores):
    raised = jnp.exp(scores - jnp.max(scores, axis=-1, keepdims=True))
    return (raised * (1.0 / jnp.sum(raised, axis=-1, keepdims=True))).astype(bf16)


def swap_halves(x):
    return jnp.concatenate([x[:, HD:], x[:, :HD]], axis=1)


def kernel(
    lat_n, lon_n, x_hbm, gain_hbm, w_hbm, table_hbm, index_hbm, group_hbm, out_ref,
    x_ref, w_ref, gain_ref, table_ref, index_ref, group_ref, own, halo, q_ref, kv_ref, bias_ref, cap_send, cap_recv, ret_send, ret_recv, acc,
    load_sem, hs_sem, hr_sem, cs_sem, cr_sem, rs_sem, rr_sem,
):
    lat, lon = lax.axis_index("lat"), lax.axis_index("lon")
    west, east = lax.rem(lon + lon_n - 1, lon_n), lax.rem(lon + 1, lon_n)
    has_n, has_s = lat > 0, lat < lat_n - 1
    polar = (lat == 0) | (lat == lat_n - 1)
    x_copy = pltpu.make_async_copy(x_hbm, x_ref, load_sem.at[0])
    w_copy = pltpu.make_async_copy(w_hbm, w_ref, load_sem.at[1])
    gain_copy = pltpu.make_async_copy(gain_hbm, gain_ref, load_sem.at[2])
    table_copy = pltpu.make_async_copy(table_hbm, table_ref, load_sem.at[3])
    index_copy = pltpu.make_async_copy(index_hbm, index_ref, load_sem.at[4])
    group_copy = pltpu.make_async_copy(group_hbm, group_ref, load_sem.at[5])
    for c in (x_copy, gain_copy, w_copy, index_copy, table_copy, group_copy):
        c.start()

    barrier = pltpu.get_barrier_semaphore()

    def greet(a, o):
        pl.semaphore_signal(barrier, inc=1, device_id=(a, o), device_id_type=MESH)

    greet(lat, west)
    greet(lat, east)

    @pl.when(has_n)
    def _():
        for o in (west, lon, east):
            greet(lat - 1, o)

    @pl.when(has_s)
    def _():
        for o in (west, lon, east):
            greet(lat + 1, o)

    @pl.when(polar)
    def _():
        @pl.loop(2, lon_n - 1)
        def _(o):
            greet(lat, lax.rem(lon + o, lon_n))

    x_copy.wait()
    own[...] = dot(one_hot(2 * STRIP, 2 * STRIP, grid_token), x_ref[...]).astype(bf16)

    as_int = lambda flag: jnp.where(flag, 1, 0)
    pl.semaphore_wait(
        barrier, 2 + 3 * as_int(has_n) + 3 * as_int(has_s) + (lon_n - 3) * as_int(polar)
    )

    def halo_copy(slot, source, target, rows, a, o):
        return pltpu.make_async_remote_copy(
            src_ref=own.at[pl.ds(source, rows)],
            dst_ref=halo.at[pl.ds(target, rows)],
            send_sem=hs_sem.at[slot],
            recv_sem=hr_sem.at[slot],
            device_id=(a, o),
            device_id_type=MESH,
        )

    last = STRIP - QUAD
    north = [
        halo_copy(0, 0, EXT + QUAD, STRIP, lat - 1, lon),
        halo_copy(1, 0, EXT + EXT - QUAD, QUAD, lat - 1, west),
        halo_copy(2, last, EXT, QUAD, lat - 1, east),
    ]
    south = [
        halo_copy(3, STRIP, QUAD, STRIP, lat + 1, lon),
        halo_copy(4, STRIP, EXT - QUAD, QUAD, lat + 1, west),
        halo_copy(5, STRIP + last, 0, QUAD, lat + 1, east),
    ]
    sides = [
        halo_copy(6, 0, 2 * EXT + 2 * QUAD, QUAD, lat, west),
        halo_copy(7, STRIP, 2 * EXT + 3 * QUAD, QUAD, lat, west),
        halo_copy(8, last, 2 * EXT, QUAD, lat, east),
        halo_copy(9, STRIP + last, 2 * EXT + QUAD, QUAD, lat, east),
    ]

    @pl.when(has_n)
    def _():
        for c in north:
            c.start()

    @pl.when(has_s)
    def _():
        for c in south:
            c.start()

    for c in sides:
        c.start()

    gain_copy.wait()
    gain = gain_ref[...]
    cap_strip = jnp.where(lat == lat_n - 1, 1, 0)

    def project(strip, wait):
        rows = pl.ds(pl.multiple_of(strip * STRIP, STRIP), STRIP)
        normed = layer_norm(own[rows], gain)
        if wait:
            w_copy.wait()
        q_ref[rows] = (dot(normed, w_ref[:, :HW]).astype(bf16) * HD ** (-0.5)).astype(bf16)
        got = dot(normed, w_ref[:, HW:]).astype(bf16)
        kv_ref[1 + strip, QUAD : QUAD + STRIP] = got

    project(cap_strip, True)
    for c in (index_copy, table_copy, group_copy):
        c.wait()

    head0 = lax.rem(lon, HEADS)
    base = lon - head0

    def cap_copy(o):
        d = lax.rem(lon + o, lon_n)
        return pltpu.make_async_remote_copy(
            src_ref=cap_send.at[lax.rem(d, HEADS)],
            dst_ref=cap_recv.at[lon],
            send_sem=cs_sem.at[o],
            recv_sem=cr_sem.at[o],
            device_id=(lat, d),
            device_id_type=MESH,
        )

    def ret_copy(j):
        d = base + lax.rem(head0 + j, HEADS)
        return pltpu.make_async_remote_copy(
            src_ref=ret_send.at[j],
            dst_ref=ret_recv.at[head0],
            send_sem=rs_sem.at[j],
            recv_sem=rr_sem.at[j],
            device_id=(lat, d),
            device_id_type=MESH,
        )

    def cap_pack(strip):
        rows = pl.ds(pl.multiple_of(strip * STRIP, STRIP), STRIP)
        lane = lax.broadcasted_iota(jnp.int32, (8, STRIP), 1)
        block = lax.broadcasted_iota(jnp.int32, (8, STRIP), 0)
        spread = jnp.where(lane // QUAD == block, 1.0, 0.0).astype(bf16)
        ids = jnp.zeros((1, STRIP), f32)
        for t in range(4):
            row = group_ref[strip, t].astype(f32).astype(bf16)
            row = dot(jnp.broadcast_to(row, (8, 8)), spread)[:1]
            ids = jnp.where((lane[:1] // 4) % 4 == t, row, ids)
        ids = jnp.broadcast_to(ids, (QUAD, STRIP)).astype(bf16)
        for h in range(HEADS):
            k = kv_ref[1 + strip, QUAD : QUAD + STRIP, h * HD : (h + 1) * HD]
            v = kv_ref[1 + strip, QUAD : QUAD + STRIP, HW + h * HD : HW + (h + 1) * HD]
            q = q_ref[rows, h * HD : (h + 1) * HD]
            cap_send[h, :STRIP] = jnp.concatenate([k, v], axis=1)
            cap_send[h, STRIP : STRIP + HD] = jnp.concatenate([q[:HD], q[HD:]], axis=1)
            cap_send[h, STRIP + HD :] = ids

    @pl.when(polar)
    def _():
        cap_pack(cap_strip)

        @pl.loop(1, lon_n)
        def _(o):
            cap_copy(o).start()

        cap_recv[lon] = cap_send[head0]

    project(1 - cap_strip, False)

    order = one_hot(64, 64, window_position)
    index = index_ref[...].astype(f32).astype(bf16)
    index = dot_t(dot(order, index).astype(bf16), order).astype(jnp.int32)
    index = jnp.concatenate([index, index], axis=1)
    table = table_ref[...]
    table_low = table[:, :128]
    table_high = jnp.concatenate(
        [table[:, 128:], jnp.zeros((HEADS, 256 - table.shape[1]), f32)], axis=1
    )
    key = lax.broadcasted_iota(jnp.int32, (64, 64), 1)
    for h in range(HEADS):
        low = jnp.take_along_axis(
            jnp.broadcast_to(table_low[h : h + 1], (64, 128)), index & 127, axis=1,
            mode="promise_in_bounds",
        )
        high = jnp.take_along_axis(
            jnp.broadcast_to(table_high[h : h + 1], (64, 128)), index & 127, axis=1,
            mode="promise_in_bounds",
        )
        bias = jnp.where(index < 128, low, high)[:, :64]
        at = (h % 2) * 32
        north_bias = jnp.where((key < 32) & (lat == 0), masked_score, bias)
        south_bias = jnp.where((key >= 32) & (lat == lat_n - 1), masked_score, bias)
        bias_ref[0, h // 2, at : at + 32] = north_bias[32:]
        bias_ref[1, h // 2, at : at + 32] = south_bias[:32]

    left = lax.broadcasted_iota(jnp.int32, (1, 128), 1) < HD

    @pl.when(polar)
    def _():
        @pl.loop(1, lon_n)
        def _(o):
            cap_copy(o).wait_recv()

        kv = jnp.concatenate([cap_recv[t, :STRIP] for t in range(lon_n)], axis=0)
        key_group = jnp.concatenate(
            [cap_recv[t, STRIP + HD :].astype(f32)[:1] for t in range(lon_n)], axis=1
        )
        diagonal = lax.broadcasted_iota(jnp.int32, (STRIP, STRIP), 0) == lax.broadcasted_iota(
            jnp.int32, (STRIP, STRIP), 1
        )

        def block(s):
            packed = cap_recv[s, STRIP : STRIP + HD].astype(f32)
            q = jnp.concatenate([packed, swap_halves(packed)], axis=0)
            q = jnp.where(left, q, 0.0).astype(bf16)
            ids = cap_recv[s, STRIP + HD :].astype(f32)[:1]
            group = jnp.sum(jnp.where(diagonal, ids, 0.0), axis=1, keepdims=True)
            scores = jnp.where(group == key_group, dot_t(q, kv), masked_score)
            result = dot(softmax_bf16(scores), kv)
            return jnp.where(left, swap_halves(result[:HD]), result[HD:]).astype(bf16)

        @pl.loop(1, HEADS)
        def _(j):
            ret_send[j] = block(base + lax.rem(head0 + j, HEADS))
            ret_copy(j).start()

        ret_recv[head0] = block(lon)

    @pl.when(has_n)
    def _():
        for c in south:
            c.wait_recv()

    @pl.when(has_s)
    def _():
        for c in north:
            c.wait_recv()

    for c in sides:
        c.wait_recv()

    @pl.when(jnp.logical_not(has_n))
    def _():
        halo[:EXT] = jnp.zeros((EXT, halo.shape[1]), bf16)

    @pl.when(jnp.logical_not(has_s))
    def _():
        halo[EXT : 2 * EXT] = jnp.zeros((EXT, halo.shape[1]), bf16)

    normed = layer_norm(halo[...], gain)
    for part in range(2):
        columns = slice(part * HW, (part + 1) * HW)
        got = dot(normed, w_ref[:, (part + 1) * HW : (part + 2) * HW]).astype(bf16)
        kv_ref[0, :, columns] = got[:EXT]
        kv_ref[3, :, columns] = got[EXT : 2 * EXT]
        for s in range(2):
            at = 2 * EXT + s * QUAD
            kv_ref[1 + s, :QUAD, columns] = got[at : at + QUAD]
            kv_ref[1 + s, EXT - QUAD :, columns] = got[at + 2 * QUAD : at + 3 * QUAD]

    keep = [jnp.where(left, 1.0, 0.0).astype(bf16), jnp.where(left, 0.0, 1.0).astype(bf16)]
    for a in range(2):
        spans, scores, values = [], [], []
        for w in range(5):
            if w == 0:
                first, count, skip = 0, QUAD, QUAD
            elif w == 4:
                first, count, skip = STRIP - QUAD, QUAD, 0
            else:
                first, count, skip = QUAD + 32 * (w - 1), 32, 0
            first += a * STRIP
            rows = slice(32 * w, 32 * w + 32)
            for pair in range(PAIRS):
                lanes = slice(pair * 128, (pair + 1) * 128)
                v_lanes = slice(HW + pair * 128, HW + (pair + 1) * 128)
                k = jnp.concatenate([kv_ref[2 * a, rows, lanes], kv_ref[2 * a + 1, rows, lanes]], axis=0)
                v = jnp.concatenate(
                    [kv_ref[2 * a, rows, v_lanes], kv_ref[2 * a + 1, rows, v_lanes]], axis=0
                )
                q = q_ref[first : first + count, lanes]
                q = jnp.concatenate([q * keep[0], q * keep[1]], axis=0)
                bias = jnp.concatenate(
                    [
                        bias_ref[a, pair, skip : skip + count],
                        bias_ref[a, pair, 32 + skip : 32 + skip + count],
                    ],
                    axis=0,
                )
                spans.append((first, count, lanes))
                scores.append(dot_t(q, k) + bias)
                values.append(v)
        scores = jnp.concatenate(scores, axis=0)
        raised = jnp.exp(scores - jnp.max(scores, axis=-1, keepdims=True))
        inverse = 1.0 / jnp.sum(raised, axis=-1, keepdims=True)
        raised = raised.astype(bf16)
        at = 0
        for (first, count, lanes), v in zip(spans, values):
            result = dot(raised[at : at + 2 * count], v) * inverse[at : at + 2 * count]
            acc[first : first + count, lanes] = jnp.where(left, result[:count], result[count:])
            at += 2 * count

    def add_cap(strip):
        for pair in range(PAIRS):
            lanes = slice(pair * 128, (pair + 1) * 128)
            even, odd = ret_recv[2 * pair].astype(f32), ret_recv[2 * pair + 1].astype(f32)
            at = pl.multiple_of(strip * STRIP, STRIP)
            acc[pl.ds(at, HD), lanes] += jnp.where(left, even, swap_halves(odd))
            acc[pl.ds(at + HD, HD), lanes] += jnp.where(left, swap_halves(even), odd)

    @pl.when(polar)
    def _():
        @pl.loop(1, HEADS)
        def _(j):
            ret_copy(j).wait_recv()

        add_cap(cap_strip)

    mixed = acc[...].astype(bf16)
    out_ref[...] = dot(one_hot(2 * STRIP, 2 * STRIP, block_token), mixed).astype(bf16)

    @pl.when(has_n)
    def _():
        for c in north:
            c.wait_send()

    @pl.when(has_s)
    def _():
        for c in south:
            c.wait_send()

    for c in sides:
        c.wait_send()

    @pl.when(polar)
    def _():
        @pl.loop(1, lon_n)
        def _(o):
            cap_copy(o).wait_send()

        @pl.loop(1, HEADS)
        def _(j):
            ret_copy(j).wait_send()


def local(tokens, ln_gain, w_qkv, bias_table, bias_index, cap_group):
    lat_n, lon_n = lax.axis_size("lat"), lax.axis_size("lon")
    rows, columns, width = tokens.shape
    count = rows * columns
    vmem = pl.BlockSpec(memory_space=pltpu.VMEM)
    hbm = pl.BlockSpec(memory_space=pltpu.HBM)
    groups = cap_group.transpose(0, 2, 3, 1)
    out = pl.pallas_call(
        functools.partial(kernel, lat_n, lon_n),
        out_shape=jax.ShapeDtypeStruct((count, HW), bf16),
        in_specs=[hbm] * 6,
        out_specs=vmem,
        scratch_shapes=[
            pltpu.VMEM((count, width), bf16),
            pltpu.VMEM(w_qkv.shape, bf16),
            pltpu.VMEM((1, width), f32),
            pltpu.VMEM(bias_table.shape, f32),
            pltpu.VMEM(bias_index.shape, jnp.int32),
            pltpu.VMEM(groups.shape, jnp.int32),
            pltpu.VMEM((count, width), bf16),
            pltpu.VMEM((2 * EXT + 4 * QUAD, width), bf16),
            pltpu.VMEM((count, HW), bf16),
            pltpu.VMEM((4, EXT, 2 * HW), bf16),
            pltpu.VMEM((2, PAIRS, 64, 64), f32),
            pltpu.VMEM((HEADS, STRIP + HD + QUAD, 128), bf16),
            pltpu.VMEM((lon_n, STRIP + HD + QUAD, 128), bf16),
            pltpu.VMEM((HEADS, HD, 128), bf16),
            pltpu.VMEM((HEADS, HD, 128), bf16),
            pltpu.VMEM((count, HW), f32),
            pltpu.SemaphoreType.DMA((6,)),
            pltpu.SemaphoreType.DMA((10,)),
            pltpu.SemaphoreType.DMA((10,)),
            pltpu.SemaphoreType.DMA((lon_n,)),
            pltpu.SemaphoreType.DMA((lon_n,)),
            pltpu.SemaphoreType.DMA((HEADS,)),
            pltpu.SemaphoreType.DMA((HEADS,)),
        ],
        compiler_params=pltpu.CompilerParams(
            collective_id=0, has_side_effects=True, vmem_limit_bytes=63 * 1024 * 1024
        ),
    )(
        tokens.reshape(count, width), ln_gain.reshape(1, width), w_qkv, bias_table, bias_index,
        groups,
    )
    return out.reshape(rows, columns, HW)


def solution(mesh):
    placed = (P("lat", "lon", None), P(), P(), P(), P(), P(None, "lon", None, None))
    return jax.shard_map(
        local, mesh=mesh, in_specs=placed, out_specs=P("lat", "lon", None), check_vma=False
    )
```

```python
import functools

import jax
import jax.numpy as jnp
from jax import lax
from jax.experimental import pallas as pl
from jax.experimental.pallas import tpu as pltpu
from jax.sharding import PartitionSpec as P

MESH = pl.DeviceIdType.MESH
HEADS = 8
HD = 64
HW = 512
STRIP = 128
QUAD = 16
EXT = STRIP + 2 * QUAD
PAIRS = HEADS // 2
epsilon = 1e-05
masked_score = -1e30
f32, bf16 = jnp.float32, jnp.bfloat16


def one_hot(rows, columns, source):
    row = lax.broadcasted_iota(jnp.int32, (rows, columns), 0)
    column = lax.broadcasted_iota(jnp.int32, (rows, columns), 1)
    return jnp.where(source(row) == column, 1.0, 0.0).astype(bf16)


def grid_token(n):
    strip, block, row, column = n // STRIP, (n // QUAD) % 8, (n // 4) % 4, n % 4
    return (strip * 4 + row) * 32 + block * 4 + column


def block_token(n):
    row, column = n // 32, n % 32
    return (row // 4) * STRIP + (column // 4) * QUAD + (row % 4) * 4 + column % 4


def window_position(n):
    high, side, row, column = n // 32, (n // QUAD) % 2, (n // 4) % 4, n % 4
    return (high * 4 + row) * 8 + side * 4 + column


def dot(a, b):
    return jnp.dot(a, b, preferred_element_type=f32)


def dot_t(a, b):
    return lax.dot_general(a, b, (((1,), (1,)), ((), ())), preferred_element_type=f32)


def layer_norm(x, gain):
    values = x.astype(f32)
    center = jnp.mean(values, axis=-1, keepdims=True)
    values = values - center
    spread = jnp.mean(values * values, axis=-1, keepdims=True)
    return (values * lax.rsqrt(spread + epsilon) * gain).astype(bf16)


def swap_halves(x):
    return jnp.concatenate([x[:, HD:], x[:, :HD]], axis=1)


def kernel(
    lat_n, lon_n, x_hbm, gain_hbm, w_hbm, table_hbm, index_hbm, group_hbm, out_ref,
    x_ref, w_ref, gain_ref, table_ref, index_ref, group_ref, own, halo, q_ref, kv_ref, bias_ref, cap_send, cap_recv, ret_send, ret_recv, acc,
    load_sem, hs_sem, hr_sem, cs_sem, cr_sem, rs_sem, rr_sem,
):
    lat, lon = lax.axis_index("lat"), lax.axis_index("lon")
    west, east = lax.rem(lon + lon_n - 1, lon_n), lax.rem(lon + 1, lon_n)
    has_n, has_s = lat > 0, lat < lat_n - 1
    polar = (lat == 0) | (lat == lat_n - 1)
    x_copy = pltpu.make_async_copy(x_hbm, x_ref, load_sem.at[0])
    w_copy = pltpu.make_async_copy(w_hbm, w_ref, load_sem.at[1])
    gain_copy = pltpu.make_async_copy(gain_hbm, gain_ref, load_sem.at[2])
    table_copy = pltpu.make_async_copy(table_hbm, table_ref, load_sem.at[3])
    index_copy = pltpu.make_async_copy(index_hbm, index_ref, load_sem.at[4])
    group_copy = pltpu.make_async_copy(group_hbm, group_ref, load_sem.at[5])
    for c in (x_copy, gain_copy, w_copy, index_copy, table_copy, group_copy):
        c.start()

    barrier = pltpu.get_barrier_semaphore()

    def greet(a, o):
        pl.semaphore_signal(barrier, inc=1, device_id=(a, o), device_id_type=MESH)

    greet(lat, west)
    greet(lat, east)

    @pl.when(has_n)
    def _():
        for o in (west, lon, east):
            greet(lat - 1, o)

    @pl.when(has_s)
    def _():
        for o in (west, lon, east):
            greet(lat + 1, o)

    @pl.when(polar)
    def _():
        @pl.loop(2, lon_n - 1)
        def _(o):
            greet(lat, lax.rem(lon + o, lon_n))

    x_copy.wait()
    own[...] = dot(one_hot(2 * STRIP, 2 * STRIP, grid_token), x_ref[...]).astype(bf16)

    as_int = lambda flag: jnp.where(flag, 1, 0)
    pl.semaphore_wait(
        barrier, 2 + 3 * as_int(has_n) + 3 * as_int(has_s) + (lon_n - 3) * as_int(polar)
    )

    def halo_copy(slot, source, target, rows, a, o):
        return pltpu.make_async_remote_copy(
            src_ref=own.at[pl.ds(source, rows)],
            dst_ref=halo.at[pl.ds(target, rows)],
            send_sem=hs_sem.at[slot],
            recv_sem=hr_sem.at[slot],
            device_id=(a, o),
            device_id_type=MESH,
        )

    last = STRIP - QUAD
    north = [
        halo_copy(0, 0, EXT + QUAD, STRIP, lat - 1, lon),
        halo_copy(1, 0, EXT + EXT - QUAD, QUAD, lat - 1, west),
        halo_copy(2, last, EXT, QUAD, lat - 1, east),
    ]
    south = [
        halo_copy(3, STRIP, QUAD, STRIP, lat + 1, lon),
        halo_copy(4, STRIP, EXT - QUAD, QUAD, lat + 1, west),
        halo_copy(5, STRIP + last, 0, QUAD, lat + 1, east),
    ]
    sides = [
        halo_copy(6, 0, 2 * EXT + 2 * QUAD, QUAD, lat, west),
        halo_copy(7, STRIP, 2 * EXT + 3 * QUAD, QUAD, lat, west),
        halo_copy(8, last, 2 * EXT, QUAD, lat, east),
        halo_copy(9, STRIP + last, 2 * EXT + QUAD, QUAD, lat, east),
    ]

    @pl.when(has_n & (lat != 1))
    def _():
        for c in north:
            c.start()

    @pl.when(has_s)
    def _():
        for c in south:
            c.start()

    @pl.when(lat == 1)
    def _():
        for c in north:
            c.start()

    for c in sides:
        c.start()

    gain_copy.wait()
    gain = gain_ref[...]
    cap_strip = jnp.where(lat == lat_n - 1, 1, 0)

    def project(strip, wait):
        rows = pl.ds(pl.multiple_of(strip * STRIP, STRIP), STRIP)
        normed = layer_norm(own[rows], gain)
        if wait:
            w_copy.wait()
        q_ref[rows] = (dot(normed, w_ref[:, :HW]).astype(bf16) * HD ** (-0.5)).astype(bf16)
        got = dot(normed, w_ref[:, HW:]).astype(bf16)
        kv_ref[1 + strip, QUAD : QUAD + STRIP] = got

    project(cap_strip, True)
    for c in (index_copy, table_copy, group_copy):
        c.wait()

    head0 = lax.rem(lon, HEADS)
    base = lon - head0

    def cap_copy(o):
        d = lax.rem(lon + o, lon_n)
        return pltpu.make_async_remote_copy(
            src_ref=cap_send.at[lax.rem(d, HEADS)],
            dst_ref=cap_recv.at[lon],
            send_sem=cs_sem.at[o],
            recv_sem=cr_sem.at[o],
            device_id=(lat, d),
            device_id_type=MESH,
        )

    def ret_copy(j):
        d = base + lax.rem(head0 + j, HEADS)
        return pltpu.make_async_remote_copy(
            src_ref=ret_send.at[j],
            dst_ref=ret_recv.at[head0],
            send_sem=rs_sem.at[j],
            recv_sem=rr_sem.at[j],
            device_id=(lat, d),
            device_id_type=MESH,
        )

    def cap_pack(strip):
        rows = pl.ds(pl.multiple_of(strip * STRIP, STRIP), STRIP)
        lane = lax.broadcasted_iota(jnp.int32, (8, STRIP), 1)
        block = lax.broadcasted_iota(jnp.int32, (8, STRIP), 0)
        spread = jnp.where(lane // QUAD == block, 1.0, 0.0).astype(bf16)
        ids = jnp.zeros((1, STRIP), f32)
        for t in range(4):
            row = group_ref[strip, t].astype(f32).astype(bf16)
            row = dot(jnp.broadcast_to(row, (8, 8)), spread)[:1]
            ids = jnp.where((lane[:1] // 4) % 4 == t, row, ids)
        ids = jnp.broadcast_to(ids, (QUAD, STRIP)).astype(bf16)
        for h in range(HEADS):
            k = kv_ref[1 + strip, QUAD : QUAD + STRIP, h * HD : (h + 1) * HD]
            v = kv_ref[1 + strip, QUAD : QUAD + STRIP, HW + h * HD : HW + (h + 1) * HD]
            q = q_ref[rows, h * HD : (h + 1) * HD]
            cap_send[h, :STRIP] = jnp.concatenate([k, v], axis=1)
            cap_send[h, STRIP : STRIP + HD] = jnp.concatenate([q[:HD], q[HD:]], axis=1)
            cap_send[h, STRIP + HD :] = ids

    @pl.when(polar)
    def _():
        cap_pack(cap_strip)

        @pl.loop(0, lon_n - 1)
        def _(k):
            cap_copy(k + 1).start()

        cap_recv[lon] = cap_send[head0]

    project(1 - cap_strip, False)

    order = one_hot(64, 64, window_position)
    index = index_ref[...].astype(f32).astype(bf16)
    index = dot_t(dot(order, index).astype(bf16), order).astype(jnp.int32)
    index = jnp.concatenate([index, index], axis=1)
    table = table_ref[...]
    table_low = table[:, :128]
    table_high = jnp.concatenate(
        [table[:, 128:], jnp.zeros((HEADS, 256 - table.shape[1]), f32)], axis=1
    )
    key = lax.broadcasted_iota(jnp.int32, (64, 64), 1)
    for h in range(HEADS):
        low = jnp.take_along_axis(
            jnp.broadcast_to(table_low[h : h + 1], (64, 128)), index & 127, axis=1,
            mode="promise_in_bounds",
        )
        high = jnp.take_along_axis(
            jnp.broadcast_to(table_high[h : h + 1], (64, 128)), index & 127, axis=1,
            mode="promise_in_bounds",
        )
        bias = jnp.where(index < 128, low, high)[:, :64]
        at = (h % 2) * 32
        north_bias = jnp.where((key < 32) & (lat == 0), masked_score, bias)
        south_bias = jnp.where((key >= 32) & (lat == lat_n - 1), masked_score, bias)
        bias_ref[0, h // 2, at : at + 32] = north_bias[32:]
        bias_ref[1, h // 2, at : at + 32] = south_bias[:32]

    left = lax.broadcasted_iota(jnp.int32, (1, 128), 1) < HD

    @pl.when(polar)
    def _():
        @pl.loop(1, lon_n)
        def _(o):
            cap_copy(o).wait_recv()

        kv = jnp.concatenate([cap_recv[t, :STRIP] for t in range(lon_n)], axis=0)
        key_group = jnp.concatenate(
            [cap_recv[t, STRIP + HD :].astype(f32)[:1] for t in range(lon_n)], axis=1
        )
        diagonal = lax.broadcasted_iota(jnp.int32, (STRIP, STRIP), 0) == lax.broadcasted_iota(
            jnp.int32, (STRIP, STRIP), 1
        )

        def block(s):
            packed = cap_recv[s, STRIP : STRIP + HD].astype(f32)
            q = jnp.concatenate([packed, swap_halves(packed)], axis=0)
            q = jnp.where(left, q, 0.0).astype(bf16)
            ids = cap_recv[s, STRIP + HD :].astype(f32)[:1]
            group = jnp.sum(jnp.where(diagonal, ids, 0.0), axis=1, keepdims=True)
            scores = jnp.where(group == key_group, dot_t(q, kv), masked_score)
            raised = jnp.exp(scores - jnp.max(scores, axis=-1, keepdims=True))
            inverse = 1.0 / jnp.sum(raised, axis=-1, keepdims=True)
            result = dot(raised.astype(bf16), kv) * inverse
            return jnp.where(left, swap_halves(result[:HD]), result[HD:]).astype(bf16)

        @pl.loop(0, HEADS - 1)
        def _(k):
            j = k + 1
            ret_send[j] = block(base + lax.rem(head0 + j, HEADS))
            ret_copy(j).start()

        ret_recv[head0] = block(lon)

    @pl.when(has_n)
    def _():
        for c in south:
            c.wait_recv()

    @pl.when(has_s)
    def _():
        for c in north:
            c.wait_recv()

    for c in sides:
        c.wait_recv()

    @pl.when(jnp.logical_not(has_n))
    def _():
        halo[:EXT] = jnp.zeros((EXT, halo.shape[1]), bf16)

    @pl.when(jnp.logical_not(has_s))
    def _():
        halo[EXT : 2 * EXT] = jnp.zeros((EXT, halo.shape[1]), bf16)

    normed = layer_norm(halo[...], gain)
    for part in range(2):
        columns = slice(part * HW, (part + 1) * HW)
        got = dot(normed, w_ref[:, (part + 1) * HW : (part + 2) * HW]).astype(bf16)
        kv_ref[0, :, columns] = got[:EXT]
        kv_ref[3, :, columns] = got[EXT : 2 * EXT]
        for s in range(2):
            at = 2 * EXT + s * QUAD
            kv_ref[1 + s, :QUAD, columns] = got[at : at + QUAD]
            kv_ref[1 + s, EXT - QUAD :, columns] = got[at + 2 * QUAD : at + 3 * QUAD]

    keep = [jnp.where(left, 1.0, 0.0).astype(bf16), jnp.where(left, 0.0, 1.0).astype(bf16)]
    for a in range(2):
        spans, scores, values = [], [], []
        for w in range(5):
            if w == 0:
                first, count, skip = 0, QUAD, QUAD
            elif w == 4:
                first, count, skip = STRIP - QUAD, QUAD, 0
            else:
                first, count, skip = QUAD + 32 * (w - 1), 32, 0
            first += a * STRIP
            rows = slice(32 * w, 32 * w + 32)
            for pair in range(PAIRS):
                lanes = slice(pair * 128, (pair + 1) * 128)
                v_lanes = slice(HW + pair * 128, HW + (pair + 1) * 128)
                k = jnp.concatenate([kv_ref[2 * a, rows, lanes], kv_ref[2 * a + 1, rows, lanes]], axis=0)
                v = jnp.concatenate(
                    [kv_ref[2 * a, rows, v_lanes], kv_ref[2 * a + 1, rows, v_lanes]], axis=0
                )
                q = q_ref[first : first + count, lanes]
                q = jnp.concatenate([q * keep[0], q * keep[1]], axis=0)
                bias = jnp.concatenate(
                    [
                        bias_ref[a, pair, skip : skip + count],
                        bias_ref[a, pair, 32 + skip : 32 + skip + count],
                    ],
                    axis=0,
                )
                spans.append((first, count, lanes))
                scores.append(dot_t(q, k) + bias)
                values.append(v)
        scores = jnp.concatenate(scores, axis=0)
        raised = jnp.exp(scores - jnp.max(scores, axis=-1, keepdims=True))
        inverse = 1.0 / jnp.sum(raised, axis=-1, keepdims=True)
        raised = raised.astype(bf16)
        at = 0
        for (first, count, lanes), v in zip(spans, values):
            result = dot(raised[at : at + 2 * count], v) * inverse[at : at + 2 * count]
            acc[first : first + count, lanes] = jnp.where(left, result[:count], result[count:])
            at += 2 * count

    def add_cap(strip):
        for pair in range(PAIRS):
            lanes = slice(pair * 128, (pair + 1) * 128)
            even, odd = ret_recv[2 * pair].astype(f32), ret_recv[2 * pair + 1].astype(f32)
            at = pl.multiple_of(strip * STRIP, STRIP)
            acc[pl.ds(at, HD), lanes] += jnp.where(left, even, swap_halves(odd))
            acc[pl.ds(at + HD, HD), lanes] += jnp.where(left, swap_halves(even), odd)

    @pl.when(polar)
    def _():
        @pl.loop(1, HEADS)
        def _(j):
            ret_copy(j).wait_recv()

        add_cap(cap_strip)

    mixed = acc[...].astype(bf16)
    out_ref[...] = dot(one_hot(2 * STRIP, 2 * STRIP, block_token), mixed).astype(bf16)

    @pl.when(has_n)
    def _():
        for c in north:
            c.wait_send()

    @pl.when(has_s)
    def _():
        for c in south:
            c.wait_send()

    for c in sides:
        c.wait_send()

    @pl.when(polar)
    def _():
        @pl.loop(1, lon_n)
        def _(o):
            cap_copy(o).wait_send()

        @pl.loop(1, HEADS)
        def _(j):
            ret_copy(j).wait_send()


def local(tokens, ln_gain, w_qkv, bias_table, bias_index, cap_group):
    lat_n, lon_n = lax.axis_size("lat"), lax.axis_size("lon")
    rows, columns, width = tokens.shape
    count = rows * columns
    vmem = pl.BlockSpec(memory_space=pltpu.VMEM)
    hbm = pl.BlockSpec(memory_space=pltpu.HBM)
    groups = cap_group.transpose(0, 2, 3, 1)
    out = pl.pallas_call(
        functools.partial(kernel, lat_n, lon_n),
        out_shape=jax.ShapeDtypeStruct((count, HW), bf16),
        in_specs=[hbm] * 6,
        out_specs=vmem,
        scratch_shapes=[
            pltpu.VMEM((count, width), bf16),
            pltpu.VMEM(w_qkv.shape, bf16),
            pltpu.VMEM((1, width), f32),
            pltpu.VMEM(bias_table.shape, f32),
            pltpu.VMEM(bias_index.shape, jnp.int32),
            pltpu.VMEM(groups.shape, jnp.int32),
            pltpu.VMEM((count, width), bf16),
            pltpu.VMEM((2 * EXT + 4 * QUAD, width), bf16),
            pltpu.VMEM((count, HW), bf16),
            pltpu.VMEM((4, EXT, 2 * HW), bf16),
            pltpu.VMEM((2, PAIRS, 64, 64), f32),
            pltpu.VMEM((HEADS, STRIP + HD + QUAD, 128), bf16),
            pltpu.VMEM((lon_n, STRIP + HD + QUAD, 128), bf16),
            pltpu.VMEM((HEADS, HD, 128), bf16),
            pltpu.VMEM((HEADS, HD, 128), bf16),
            pltpu.VMEM((count, HW), f32),
            pltpu.SemaphoreType.DMA((6,)),
            pltpu.SemaphoreType.DMA((10,)),
            pltpu.SemaphoreType.DMA((10,)),
            pltpu.SemaphoreType.DMA((lon_n,)),
            pltpu.SemaphoreType.DMA((lon_n,)),
            pltpu.SemaphoreType.DMA((HEADS,)),
            pltpu.SemaphoreType.DMA((HEADS,)),
        ],
        compiler_params=pltpu.CompilerParams(
            collective_id=0, has_side_effects=True, vmem_limit_bytes=63 * 1024 * 1024
        ),
    )(
        tokens.reshape(count, width), ln_gain.reshape(1, width), w_qkv, bias_table, bias_index,
        groups,
    )
    return out.reshape(rows, columns, HW)


def solution(mesh):
    placed = (P("lat", "lon", None), P(), P(), P(), P(), P(None, "lon", None, None))
    return jax.shard_map(
        local, mesh=mesh, in_specs=placed, out_specs=P("lat", "lon", None), check_vma=False
    )
```
